32 devices in a mesh: groups: 2 (over x), rows: 16 (over z, y, core).
Axes of the slice: x: 2, y: 2, z: 4, core: 2. Of those that a mesh axis runs over, the one named last changes fastest.
Arguments:
- features: float32 [65536, 128], P(('groups', 'rows')), parts along dimension 0, may hold values from -6 to 6
- landmark_index: int32 [2048], P('groups'), parts along dimension 0, may hold values from 0 to 32767, as said below
- noise: float32 [1], replicated, may hold values from 0.5 to 2
- length_inv: float32 [128], replicated, may hold values from 0.6 to 1.4
- probe_bits: int32 [16, 65536], P(None, ('groups', 'rows')), parts along dimension 1, may hold values from 0 to 1
Outputs:
- preconditioned: float32 [16, 65536], P(None, ('groups', 'rows')), parts along dimension 1
The draws below stay inside these ranges and needn't reach their ends.
There are 2 independent parts, one for each index of `groups`. The reference program is written for one: setup_inputs(seed, part) draws one part's arguments, and reference() takes and returns one part's arrays. A program takes and returns all parts, laid end to end along the dimension named above; an argument that names none is the same for every part. Nothing has to cross between parts.
Inputs may be any that keep to these rules, and one draw needn't show every extreme that they name: `landmark_index`: distinct rows; at most 256 of them lie among one device's 2048 consecutive rows, and some device holds exactly 256.
All inputs are finite; a program needn't handle non-finite values.
Results may differ from the reference program's by a relative error of at most 0.006.
Values sent between devices are 32-bit elements; how exact they have to be, the bound alone decides.
A program may use at most 128 MiB of HBM per device.

```python
import math
import jax
import jax.numpy as jnp
from jax import lax

F = 128
M = 1024
PROBES = 16
ROWS_DEV = 2048
NPTS = 32768
LMAX = 256


def draw_landmark_index(key, part):
    key = jax.random.fold_in(key, 11)
    owners = NPTS // ROWS_DEV
    key_level, key_top, key_noise, key_offset = jax.random.split(key, 4)
    level = jax.random.randint(key_level, (owners,), 0, 4)
    busiest = jax.random.randint(key_top, (), 0, owners)
    level = jnp.where(jnp.arange(owners) == busiest, 8, level)
    jitter = jax.random.randint(key_noise, (owners, LMAX), 0, 1024)
    places = jnp.arange(owners * LMAX, dtype=jnp.int32).reshape(owners, LMAX)
    score = (level[:, None] * 1024 + jitter) * (owners * LMAX) + places
    _, picked = lax.top_k(score.reshape(-1), M)
    owner = picked // LMAX
    slot = picked % LMAX
    stride = ROWS_DEV // LMAX
    offset = jax.random.randint(key_offset, (M,), 0, stride)
    return (owner * ROWS_DEV + slot * stride + offset).astype(jnp.int32)


def set_ends(array, own_key, low, largest):
    index_at = [jax.random.randint(jax.random.fold_in(own_key, axis), (), 0, length) for axis, length in enumerate(array.shape)]
    widest = array.shape.index(max(array.shape))
    next_to = index_at[:widest] + [(index_at[widest] + 1) % array.shape[widest]] + index_at[widest + 1:]
    return array.at[tuple(index_at)].set(low).at[tuple(next_to)].set(largest)


def levels(rng, shape, shards, low, top_value):
    def one(axis_at, shards_of):
        draws = jax.random.uniform(jax.random.fold_in(jax.random.fold_in(rng, 6), axis_at), (shards_of,), jnp.float32, low / len(shards), top_value / len(shards))
        return jnp.repeat(jnp.exp(draws), shape[axis_at] // shards_of).reshape((-1,) + (1,) * (len(shape) - axis_at - 1))

    level = one(*shards[0])
    for cut in shards[1:]:
        level = level * one(*cut)
    return level


def centred(own_key, dims, deviation, most, pieces=(), kind=jnp.bfloat16):
    array = deviation * jax.random.normal(own_key, dims, jnp.float32)
    if pieces:
        array = array * levels(own_key, dims, pieces, -0.22, 0.18)
    return jnp.clip(array, -most, most).astype(kind)


def setup_inputs(seed: int = 0, part: int = 0) -> dict:
    streams_of = jax.random.split(jax.random.key(seed), 6)
    own_keys = jax.random.split(jax.random.fold_in(streams_of[5], part), 6)
    return {
        "features": centred(own_keys[0], (NPTS, F), 1.0, 6.0, ((0, 16),), jnp.float32),
        "landmark_index": draw_landmark_index(jax.random.fold_in(jax.random.fold_in(streams_of[5], part), 71), part),
        "noise": jnp.clip(jnp.exp(jax.random.uniform(streams_of[2], (1,), jnp.float32, math.log(0.5), math.log(2.0))), 0.5, 2.0),
        "length_inv": jnp.clip(jnp.exp(jax.random.uniform(streams_of[3], (F,), jnp.float32, math.log(0.6), math.log(1.4))), 0.6, 1.4),
        "probe_bits": set_ends(jax.random.randint(own_keys[4], (PROBES, NPTS), 0, 2), jax.random.fold_in(own_keys[4], 1), 0, 1).astype(jnp.int32),
    }


sharpness = 1.5

def scale_rows(rows, length_inv):
    return rows * length_inv[None, :]

def kernel(left, right):
    cross = jnp.dot(left.astype(jnp.float32), right.T.astype(jnp.float32), precision=lax.Precision.HIGHEST, preferred_element_type=jnp.float32)
    left_sq = jnp.sum(left * left, axis=1)
    right_sq = jnp.sum(right * right, axis=1)
    expo = sharpness * (left_sq[:, None] + right_sq[None, :] - 2.0 * cross) / left.shape[1]
    return jnp.exp(-expo)

def reference(features, landmark_index, noise, length_inv, probe_bits):
    landmarks = scale_rows(features[landmark_index], length_inv)
    inner_kernel = kernel(landmarks, landmarks)
    blocks = features.reshape(NPTS // ROWS_DEV, ROWS_DEV, F)
    signs = (2 * probe_bits - 1).astype(jnp.float32)
    sign_blocks = signs.reshape(PROBES, NPTS // ROWS_DEV, ROWS_DEV).transpose(1, 0, 2)

    def accumulate(carry, item):
        rows, sign_rows = item
        cross = kernel(scale_rows(rows, length_inv), landmarks)
        gram = carry[0] + lax.dot_general(cross.astype(jnp.float32), cross.astype(jnp.float32), (((0,), (0,)), ((), ())), precision=lax.Precision.HIGHEST, preferred_element_type=jnp.float32)
        proj = carry[1] + jnp.dot(sign_rows.astype(jnp.float32), cross.astype(jnp.float32), precision=lax.Precision.HIGHEST, preferred_element_type=jnp.float32)
        return ((gram, proj), None)
    start = (jnp.zeros((M, M), jnp.float32), jnp.zeros((PROBES, M), jnp.float32))
    (gram, projection), _ = lax.scan(accumulate, start, (blocks, sign_blocks))
    inner = noise[0] * inner_kernel + gram
    lower = jnp.linalg.cholesky(inner)
    solved = jax.scipy.linalg.cho_solve((lower, True), projection.T)

    def apply(carry, item):
        rows, sign_rows = item
        cross = kernel(scale_rows(rows, length_inv), landmarks)
        taken = jnp.dot(cross, solved, precision=lax.Precision.HIGHEST)
        return (carry, (sign_rows - taken.T) / noise[0])
    _, outs = lax.scan(apply, jnp.zeros((), jnp.float32), (blocks, sign_blocks))
    return outs.transpose(1, 0, 2).reshape(PROBES, NPTS)
```

```python
import jax
import jax.numpy as jnp
from jax import lax
from jax.experimental import pallas as pl
from jax.experimental.pallas import tpu as pltpu
from jax.sharding import PartitionSpec as P

HI = lax.Precision.HIGHEST

def mm(a, b):
    return jnp.dot(a, b, precision=HI, preferred_element_type=jnp.float32)

def mm_nt(a, b):
    return lax.dot_general(a, b, (((1,), (1,)), ((), ())), precision=HI, preferred_element_type=jnp.float32)

def invert_factor(rows):
    lane = lax.broadcasted_iota(jnp.int32, (8, 128), 1)
    sub = lax.broadcasted_iota(jnp.int32, (8, 128), 0)
    rows = list(rows)
    count = len(rows)
    result = []
    for t in range(count):
        below = range(t + 1, count)
        cols = {i: [jnp.broadcast_to(rows[i][:, 8 * t + j:8 * t + j + 1], (8, 128)) for j in range(8)] for i in range(t, count)}
        pivot = cols[t]
        inside = (lane >= 8 * t) & (lane < 8 * t + 8)
        row = jnp.where(inside, jnp.where(lane == sub + 8 * t, 1.0, 0.0), rows[t])
        root = jnp.zeros((8, 128), jnp.float32)
        spread = []
        for j in range(8):
            lead = jnp.broadcast_to(pivot[j][j:j + 1], (8, 128))
            inv = 1.0 / lead
            root = jnp.where(sub == j, lead, root)
            factor = jnp.where(sub > j, pivot[j], 0.0) * inv
            across = jnp.broadcast_to(row[j:j + 1], (8, 128))
            spread.append(across * inv)
            row = row - factor * across
            for i in range(j + 1, 8):
                entry = jnp.broadcast_to(pivot[i][j:j + 1], (8, 128))
                pivot[i] = pivot[i] - factor * entry
                ratio = entry * inv
                for m in below:
                    cols[m][i] = cols[m][i] - cols[m][j] * ratio
        for i in below:
            acc = jnp.where(inside, 0.0, rows[i])
            for j in range(8):
                acc = acc - cols[i][j] * spread[j]
            rows[i] = acc
        result.append(jnp.where(lane < 8 * t + 8, row, 0.0) * lax.rsqrt(root))
    return result

def solve_body(inner_ref, rhs_ref, out_ref, work, inverse):
    count = inner_ref.shape[0]
    extra = rhs_ref.shape[0]
    total = count + extra
    blocks = count // 128
    work[:count, :] = inner_ref[...]
    work[count:, :] = rhs_ref[...]

    def step(k, carry):
        start = pl.multiple_of(k * 128, 128)
        rows = [work[pl.ds(start + 8 * i, 8), pl.ds(start, 128)] for i in range(16)]
        rows = invert_factor(rows)
        for i in range(16):
            inverse[k, 8 * i:8 * i + 8, :] = rows[i]
        for c in range(blocks):
            @pl.when(k == c)
            def _():
                lo = 128 * (c + 1)
                scaled = mm_nt(work[lo:, 128 * c:lo], inverse[c])
                work[lo:, 128 * c:lo] = scaled
                left = lo
                while left < count:
                    right = min(count, left + 256)
                    work[left:, left:right] = work[left:, left:right] - mm_nt(scaled[left - lo:], scaled[left - lo:right - lo])
                    left = right
        return carry

    lax.fori_loop(0, blocks, step, 0)
    for k in reversed(range(blocks)):
        lo = 128 * (k + 1)
        got = work[count:, 128 * k:lo]
        if lo < count:
            got = got - mm(out_ref[:, lo:], work[lo:count, 128 * k:lo])
        out_ref[:, 128 * k:lo] = mm(got, inverse[k])

def solve_rows(inner, rhs):
    count = inner.shape[0]
    extra = rhs.shape[0]
    return pl.pallas_call(
        solve_body,
        out_shape=jax.ShapeDtypeStruct((extra, count), jnp.float32),
        in_specs=[pl.BlockSpec(memory_space=pltpu.VMEM)] * 2,
        out_specs=pl.BlockSpec(memory_space=pltpu.VMEM),
        scratch_shapes=[
            pltpu.VMEM((count + extra, count), jnp.float32),
            pltpu.VMEM((count // 128, 128, 128), jnp.float32),
        ],
        compiler_params=pltpu.CompilerParams(vmem_limit_bytes=40 * 1024 * 1024),
        cost_estimate=pl.CostEstimate(flops=2 * count ** 3, bytes_accessed=4 * count * count, transcendentals=0),
    )(inner, rhs)


sharpness = 1.5


def scale_rows(rows, length_inv):
    return rows * length_inv[None, :]


def kernel(left, right, right_sq):
    cross = jnp.dot(
        left, right.T, precision=lax.Precision.HIGHEST, preferred_element_type=jnp.float32
    )
    left_sq = jnp.sum(left * left, axis=1)
    expo = sharpness * (left_sq[:, None] + right_sq[None, :] - 2.0 * cross) / left.shape[1]
    return jnp.exp(-expo)


def outer_sum(left, right):
    return lax.dot_general(
        left,
        right,
        (((0,), (0,)), ((), ())),
        precision=lax.Precision.HIGHEST,
        preferred_element_type=jnp.float32,
    )


def local(features, landmark_index, noise, length_inv, probe_bits):
    rows_dev, width = features.shape
    count = landmark_index.shape[0]
    owner = landmark_index // rows_dev
    local_row = landmark_index - owner * rows_dev
    mine = owner == lax.axis_index("rows")
    picked = jnp.where(mine[:, None], features[local_row], 0.0)
    summed = lax.psum(picked, "rows")
    landmarks = scale_rows(summed, length_inv)
    land_sq = jnp.sum(landmarks * landmarks, axis=1)
    inner_kernel = kernel(landmarks, landmarks, land_sq)
    block = min(rows_dev, 1024)
    scaled = scale_rows(features, length_inv).reshape(rows_dev // block, block, width)

    def one_block(rows):
        return kernel(rows, landmarks, land_sq)

    cross = lax.map(one_block, scaled).reshape(rows_dev, count)
    signs = (2 * probe_bits - 1).astype(jnp.float32)
    local_proj = jnp.dot(
        signs, cross, precision=lax.Precision.HIGHEST, preferred_element_type=jnp.float32
    )
    local_gram = outer_sum(cross, cross)
    gram = lax.psum(local_gram, "rows")
    projection = lax.psum(local_proj, "rows")
    inner = noise[0] * inner_kernel + gram
    solved = solve_rows(inner, projection)
    return (signs - mm_nt(solved, cross)) / noise[0]


def solution(mesh):
    in_specs = (P(("groups", "rows"), None), P("groups"), P(), P(), P(None, ("groups", "rows")))
    out_specs = P(None, ("groups", "rows"))
    return jax.shard_map(local, mesh=mesh, in_specs=in_specs, out_specs=out_specs, check_vma=False)
```

```python
import functools

import jax
import jax.numpy as jnp
from jax import lax
from jax.experimental import pallas as pl
from jax.experimental.pallas import tpu as pltpu
from jax.sharding import PartitionSpec as P

HI = lax.Precision.HIGHEST

def mm(a, b):
    return jnp.dot(a, b, precision=HI, preferred_element_type=jnp.float32)

def mm_nt(a, b):
    return lax.dot_general(a, b, (((1,), (1,)), ((), ())), precision=HI, preferred_element_type=jnp.float32)

def invert_factor(rows):
    lane = lax.broadcasted_iota(jnp.int32, (8, 128), 1)
    sub = lax.broadcasted_iota(jnp.int32, (8, 128), 0)
    rows = list(rows)
    count = len(rows)
    result = []
    for t in range(count):
        below = range(t + 1, count)
        cols = {i: [jnp.broadcast_to(rows[i][:, 8 * t + j:8 * t + j + 1], (8, 128)) for j in range(8)] for i in range(t, count)}
        pivot = cols[t]
        inside = (lane >= 8 * t) & (lane < 8 * t + 8)
        row = jnp.where(inside, jnp.where(lane == sub + 8 * t, 1.0, 0.0), rows[t])
        root = jnp.zeros((8, 128), jnp.float32)
        spread = []
        for j in range(8):
            lead = jnp.broadcast_to(pivot[j][j:j + 1], (8, 128))
            inv = 1.0 / lead
            root = jnp.where(sub == j, lead, root)
            factor = jnp.where(sub > j, pivot[j], 0.0) * inv
            across = jnp.broadcast_to(row[j:j + 1], (8, 128))
            spread.append(across * inv)
            row = row - factor * across
            for i in range(j + 1, 8):
                entry = jnp.broadcast_to(pivot[i][j:j + 1], (8, 128))
                pivot[i] = pivot[i] - factor * entry
                ratio = entry * inv
                for m in below:
                    cols[m][i] = cols[m][i] - cols[m][j] * ratio
        for i in below:
            acc = jnp.where(inside, 0.0, rows[i])
            for j in range(8):
                acc = acc - cols[i][j] * spread[j]
            rows[i] = acc
        result.append(jnp.where(lane < 8 * t + 8, row, 0.0) * lax.rsqrt(root))
    return result

def panels(count):
    found, start = [], 0
    for left in range(0, count, 256):
        found.append((left, start, start + count - left))
        start += count - left
    return found


def solve_body(gram_ref, kern_ref, rhs_ref, out_ref, work, inverse):
    extra, count = rhs_ref.shape
    total = count + extra
    blocks = count // 128
    for left, start, stop in panels(count):
        work[left:count, left:left + 256] = gram_ref[start:stop, :] + kern_ref[start:stop, :]
    work[count:, :] = rhs_ref[...]

    def step(k, carry):
        start = pl.multiple_of(k * 128, 128)
        rows = [work[pl.ds(start + 8 * i, 8), pl.ds(start, 128)] for i in range(16)]
        rows = invert_factor(rows)
        for i in range(16):
            inverse[k, 8 * i:8 * i + 8, :] = rows[i]
        for c in range(blocks):
            @pl.when(k == c)
            def _():
                lo = 128 * (c + 1)
                scaled = mm_nt(work[lo:, 128 * c:lo], inverse[c])
                work[lo:, 128 * c:lo] = scaled
                left = lo
                while left < count:
                    right = min(count, left + 256)
                    work[left:, left:right] = work[left:, left:right] - mm_nt(scaled[left - lo:], scaled[left - lo:right - lo])
                    left = right
        return carry

    lax.fori_loop(0, blocks, step, 0)
    for k in reversed(range(blocks)):
        lo = 128 * (k + 1)
        got = work[count:, 128 * k:lo]
        if lo < count:
            got = got - mm(out_ref[:, lo:], work[lo:count, 128 * k:lo])
        out_ref[:, 128 * k:lo] = mm(got, inverse[k])

def solve_rows(gram, kern, rhs):
    extra, count = rhs.shape
    return pl.pallas_call(
        solve_body,
        out_shape=jax.ShapeDtypeStruct((extra, count), jnp.float32),
        in_specs=[pl.BlockSpec(memory_space=pltpu.VMEM)] * 3,
        out_specs=pl.BlockSpec(memory_space=pltpu.VMEM),
        scratch_shapes=[
            pltpu.VMEM((count + extra, count), jnp.float32),
            pltpu.VMEM((count // 128, 128, 128), jnp.float32),
        ],
        compiler_params=pltpu.CompilerParams(vmem_limit_bytes=40 * 1024 * 1024),
        cost_estimate=pl.CostEstimate(flops=2 * count ** 3, bytes_accessed=4 * count * count, transcendentals=0),
    )(gram, kern, rhs)


def sum_body(axis, size, data_ref, out_ref, acc, held, send_sem, recv_sem):
    chunks, rows, _ = data_ref.shape
    me = lax.axis_index(axis)
    levels = size.bit_length() - 1
    partner, bit, base = [], [], [0]
    for s in range(levels):
        stride = 1 << s
        digit = lax.rem(me // stride, 2)
        bit.append(digit)
        partner.append(me + stride - 2 * stride * digit)
        base.append(base[-1] + digit * (rows >> (s + 1)))
    barrier = pltpu.get_barrier_semaphore()
    for other in partner:
        pl.semaphore_signal(barrier, inc=1, device_id={axis: other}, device_id_type=pl.DeviceIdType.MESH)
    pl.semaphore_wait(barrier, levels)

    def span(start, length):
        return pl.ds(pl.multiple_of(start, 8), length)

    def copy(c, s):
        if s < levels:
            half = rows >> (s + 1)
            source = data_ref if s == 0 else acc
            gone = span(base[s] + (1 - bit[s]) * half, half)
            place = held.at[c, pl.ds(rows - (rows >> s), half)]
            source = source.at[c, gone]
            other = partner[s]
        else:
            level = 2 * levels - 1 - s
            part = span(base[level + 1], rows >> (level + 1))
            source = out_ref.at[c, part]
            place = out_ref.at[c, part]
            other = partner[level]
        return pltpu.make_async_remote_copy(
            src_ref=source,
            dst_ref=place,
            send_sem=send_sem.at[c, s],
            recv_sem=recv_sem.at[c, s],
            device_id={axis: other},
            device_id_type=pl.DeviceIdType.MESH,
        )

    def finish(c, s):
        copy(c, s).wait()
        if s < levels:
            half = rows >> (s + 1)
            kept = span(base[s + 1], half)
            source = data_ref if s == 0 else acc
            place = out_ref if s == levels - 1 else acc
            place[c, kept, :] = source[c, kept, :] + held[c, pl.ds(rows - (rows >> s), half), :]

    stages = 2 * levels
    for turn in range(chunks + stages):
        for c in range(chunks):
            s = turn - c
            if 0 < s <= stages:
                finish(c, s - 1)
            if 0 <= s < stages:
                copy(c, s).start()


def sum_rows(data, axis, size, chunks, number):
    rows, width = data.shape
    unit = 8 * size
    chunks = min(chunks, -(-rows // unit))
    each = -(-rows // (unit * chunks)) * unit
    padded = jnp.pad(data, ((0, each * chunks - rows), (0, 0))).reshape(chunks, each, width)
    stages = 2 * (size.bit_length() - 1)
    total = pl.pallas_call(
        functools.partial(sum_body, axis, size),
        out_shape=jax.ShapeDtypeStruct(padded.shape, jnp.float32),
        in_specs=[pl.BlockSpec(memory_space=pltpu.VMEM)],
        out_specs=pl.BlockSpec(memory_space=pltpu.VMEM),
        scratch_shapes=[
            pltpu.VMEM(padded.shape, jnp.float32),
            pltpu.VMEM(padded.shape, jnp.float32),
            pltpu.SemaphoreType.DMA((chunks, stages)),
            pltpu.SemaphoreType.DMA((chunks, stages)),
        ],
        compiler_params=pltpu.CompilerParams(
            collective_id=number, has_side_effects=True, vmem_limit_bytes=40 * 1024 * 1024
        ),
    )(padded)
    return total.reshape(each * chunks, width)[:rows]


sharpness = 1.5


def scale_rows(rows, length_inv):
    return rows * length_inv[None, :]


def kernel(left, right, right_sq):
    cross = jnp.dot(
        left, right.T, precision=lax.Precision.HIGHEST, preferred_element_type=jnp.float32
    )
    left_sq = jnp.sum(left * left, axis=1)
    expo = sharpness * (left_sq[:, None] + right_sq[None, :] - 2.0 * cross) / left.shape[1]
    return jnp.exp(-expo)


def outer_sum(left, right):
    return lax.dot_general(
        left,
        right,
        (((0,), (0,)), ((), ())),
        precision=lax.Precision.HIGHEST,
        preferred_element_type=jnp.float32,
    )


def local(size, features, landmark_index, noise, length_inv, probe_bits):
    rows_dev, width = features.shape
    count = landmark_index.shape[0]
    owner = landmark_index // rows_dev
    local_row = landmark_index - owner * rows_dev
    mine = owner == lax.axis_index("rows")
    picked = jnp.where(mine[:, None], features[local_row], 0.0)
    summed = sum_rows(picked, "rows", size, 1, 1)
    landmarks = scale_rows(summed, length_inv)
    land_sq = jnp.sum(landmarks * landmarks, axis=1)
    scaled = scale_rows(features, length_inv)
    cross = kernel(scaled, landmarks, land_sq)
    signs = (2 * probe_bits - 1).astype(jnp.float32)
    local_proj = mm(signs, cross)
    lefts = [left for left, _, _ in panels(count)]
    parts = [outer_sum(cross[:, left:], cross[:, left:left + 256]) for left in lefts]
    parts.append(local_proj.reshape(-1, 256))
    total = sum_rows(jnp.concatenate(parts), "rows", size, 3, 2)
    packed = panels(count)[-1][2]
    kern = [
        kernel(landmarks[left:], landmarks[left:left + 256], land_sq[left:left + 256])
        for left in lefts
    ]
    kern = noise[0] * jnp.concatenate(kern)
    solved = solve_rows(total[:packed], kern, total[packed:].reshape(local_proj.shape))
    return (signs - mm_nt(solved, cross)) / noise[0]


def solution(mesh):
    in_specs = (P(("groups", "rows"), None), P("groups"), P(), P(), P(None, ("groups", "rows")))
    out_specs = P(None, ("groups", "rows"))
    return jax.shard_map(functools.partial(local, mesh.shape["rows"]), mesh=mesh, in_specs=in_specs, out_specs=out_specs, check_vma=False)
```

```python
import functools

import jax
import jax.numpy as jnp
from jax import lax
from jax.experimental import pallas as pl
from jax.experimental.pallas import tpu as pltpu
from jax.sharding import PartitionSpec as P

HI = lax.Precision.HIGHEST

def mm(a, b):
    return jnp.dot(a, b, precision=HI, preferred_element_type=jnp.float32)

def mm_nt(a, b):
    return lax.dot_general(a, b, (((1,), (1,)), ((), ())), precision=HI, preferred_element_type=jnp.float32)

def invert_factor(rows):
    lane = lax.broadcasted_iota(jnp.int32, (8, 128), 1)
    sub = lax.broadcasted_iota(jnp.int32, (8, 128), 0)
    rows = list(rows)
    count = len(rows)
    result = []
    for t in range(count):
        below = range(t + 1, count)
        cols = {i: [jnp.broadcast_to(rows[i][:, 8 * t + j:8 * t + j + 1], (8, 128)) for j in range(8)] for i in range(t, count)}
        pivot = cols[t]
        inside = (lane >= 8 * t) & (lane < 8 * t + 8)
        row = jnp.where(inside, jnp.where(lane == sub + 8 * t, 1.0, 0.0), rows[t])
        root = jnp.zeros((8, 128), jnp.float32)
        spread = []
        for j in range(8):
            lead = jnp.broadcast_to(pivot[j][j:j + 1], (8, 128))
            inv = 1.0 / lead
            root = jnp.where(sub == j, lead, root)
            factor = jnp.where(sub > j, pivot[j], 0.0) * inv
            across = jnp.broadcast_to(row[j:j + 1], (8, 128))
            spread.append(across * inv)
            row = row - factor * across
            for i in range(j + 1, 8):
                entry = jnp.broadcast_to(pivot[i][j:j + 1], (8, 128))
                pivot[i] = pivot[i] - factor * entry
                ratio = entry * inv
                for m in below:
                    cols[m][i] = cols[m][i] - cols[m][j] * ratio
        for i in below:
            acc = jnp.where(inside, 0.0, rows[i])
            for j in range(8):
                acc = acc - cols[i][j] * spread[j]
            rows[i] = acc
        result.append(jnp.where(lane < 8 * t + 8, row, 0.0) * lax.rsqrt(root))
    return result

def panels(count):
    found, start = [], 0
    for left in range(0, count, 256):
        found.append((left, start, start + count - left))
        start += count - left
    return found


def solve_body(gram_ref, kern_ref, rhs_ref, out_ref, work, inverse):
    extra, count = rhs_ref.shape
    total = count + extra
    blocks = count // 128
    for left, start, stop in panels(count):
        work[left:count, left:left + 256] = gram_ref[start:stop, :] + kern_ref[start:stop, :]
    work[count:, :] = rhs_ref[...]

    def step(k, carry):
        start = pl.multiple_of(k * 128, 128)
        rows = [work[pl.ds(start + 8 * i, 8), pl.ds(start, 128)] for i in range(16)]
        rows = invert_factor(rows)
        for i in range(16):
            inverse[k, 8 * i:8 * i + 8, :] = rows[i]
        for c in range(blocks):
            @pl.when(k == c)
            def _():
                lo = 128 * (c + 1)
                scaled = mm_nt(work[lo:, 128 * c:lo], inverse[c])
                work[lo:, 128 * c:lo] = scaled
                left = lo
                while left < count:
                    right = min(count, left + 256)
                    work[left:, left:right] = work[left:, left:right] - mm_nt(scaled[left - lo:], scaled[left - lo:right - lo])
                    left = right
        return carry

    lax.fori_loop(0, blocks, step, 0)
    for k in reversed(range(blocks)):
        lo = 128 * (k + 1)
        got = work[count:, 128 * k:lo]
        if lo < count:
            got = got - mm(out_ref[:, lo:], work[lo:count, 128 * k:lo])
        out_ref[:, 128 * k:lo] = mm(got, inverse[k])

def solve_rows(gram, kern, rhs):
    extra, count = rhs.shape
    return pl.pallas_call(
        solve_body,
        out_shape=jax.ShapeDtypeStruct((extra, count), jnp.float32),
        in_specs=[pl.BlockSpec(memory_space=pltpu.VMEM)] * 3,
        out_specs=pl.BlockSpec(memory_space=pltpu.VMEM),
        scratch_shapes=[
            pltpu.VMEM((count + extra, count), jnp.float32),
            pltpu.VMEM((count // 128, 128, 128), jnp.float32),
        ],
        compiler_params=pltpu.CompilerParams(vmem_limit_bytes=40 * 1024 * 1024),
        cost_estimate=pl.CostEstimate(flops=2 * count ** 3, bytes_accessed=4 * count * count, transcendentals=0),
    )(gram, kern, rhs)


def sum_body(axis, size, data_ref, out_ref, acc, held, send_sem, recv_sem):
    chunks, rows, _ = data_ref.shape
    me = lax.axis_index(axis)
    levels = size.bit_length() - 1
    partner, bit, base = [], [], [0]
    for s in range(levels):
        stride = 1 << s
        digit = lax.rem(me // stride, 2)
        bit.append(digit)
        partner.append(me + stride - 2 * stride * digit)
        base.append(base[-1] + digit * (rows >> (s + 1)))
    barrier = pltpu.get_barrier_semaphore()
    for other in partner:
        pl.semaphore_signal(barrier, inc=1, device_id={axis: other}, device_id_type=pl.DeviceIdType.MESH)
    pl.semaphore_wait(barrier, levels)

    def span(start, length):
        return pl.ds(pl.multiple_of(start, 8), length)

    def copy(c, s):
        if s < levels:
            half = rows >> (s + 1)
            source = data_ref if s == 0 else acc
            gone = span(base[s] + (1 - bit[s]) * half, half)
            place = held.at[c, pl.ds(rows - (rows >> s), half)]
            source = source.at[c, gone]
            other = partner[s]
        else:
            level = 2 * levels - 1 - s
            part = span(base[level + 1], rows >> (level + 1))
            source = out_ref.at[c, part]
            place = out_ref.at[c, part]
            other = partner[level]
        return pltpu.make_async_remote_copy(
            src_ref=source,
            dst_ref=place,
            send_sem=send_sem.at[c, s],
            recv_sem=recv_sem.at[c, s],
            device_id={axis: other},
            device_id_type=pl.DeviceIdType.MESH,
        )

    def finish(c, s):
        copy(c, s).wait()
        if s < levels:
            half = rows >> (s + 1)
            kept = span(base[s + 1], half)
            source = data_ref if s == 0 else acc
            place = out_ref if s == levels - 1 else acc
            place[c, kept, :] = source[c, kept, :] + held[c, pl.ds(rows - (rows >> s), half), :]

    stages = 2 * levels
    for turn in range(chunks + stages):
        for c in range(chunks):
            s = turn - c
            if 0 < s <= stages:
                finish(c, s - 1)
            if 0 <= s < stages:
                copy(c, s).start()


def sum_rows(data, axis, size, chunks, number):
    rows, width = data.shape
    unit = 8 * size
    chunks = min(chunks, -(-rows // unit))
    each = -(-rows // (unit * chunks)) * unit
    padded = jnp.pad(data, ((0, each * chunks - rows), (0, 0))).reshape(chunks, each, width)
    stages = 2 * (size.bit_length() - 1)
    total = pl.pallas_call(
        functools.partial(sum_body, axis, size),
        out_shape=jax.ShapeDtypeStruct(padded.shape, jnp.float32),
        in_specs=[pl.BlockSpec(memory_space=pltpu.VMEM)],
        out_specs=pl.BlockSpec(memory_space=pltpu.VMEM),
        scratch_shapes=[
            pltpu.VMEM(padded.shape, jnp.float32),
            pltpu.VMEM(padded.shape, jnp.float32),
            pltpu.SemaphoreType.DMA((chunks, stages)),
            pltpu.SemaphoreType.DMA((chunks, stages)),
        ],
        compiler_params=pltpu.CompilerParams(
            collective_id=number, has_side_effects=True, vmem_limit_bytes=40 * 1024 * 1024
        ),
    )(padded)
    return total.reshape(each * chunks, width)[:rows]


sharpness = 1.5


def scale_rows(rows, length_inv):
    return rows * length_inv[None, :]


def kernel(left, right, right_sq):
    cross = jnp.dot(
        left, right.T, precision=lax.Precision.HIGHEST, preferred_element_type=jnp.float32
    )
    left_sq = jnp.sum(left * left, axis=1)
    expo = sharpness * (left_sq[:, None] + right_sq[None, :] - 2.0 * cross) / left.shape[1]
    return jnp.exp(-expo)


def outer_sum(left, right):
    return lax.dot_general(
        left,
        right,
        (((0,), (0,)), ((), ())),
        precision=lax.Precision.HIGH,
        preferred_element_type=jnp.float32,
    )


def local(size, features, landmark_index, noise, length_inv, probe_bits):
    rows_dev, width = features.shape
    count = landmark_index.shape[0]
    owner = landmark_index // rows_dev
    local_row = landmark_index - owner * rows_dev
    mine = owner == lax.axis_index("rows")
    picked = jnp.where(mine[:, None], features[local_row], 0.0)
    summed = sum_rows(picked, "rows", size, 1, 1)
    landmarks = scale_rows(summed, length_inv)
    land_sq = jnp.sum(landmarks * landmarks, axis=1)
    scaled = scale_rows(features, length_inv)
    cross = kernel(scaled, landmarks, land_sq)
    signs = (2 * probe_bits - 1).astype(jnp.float32)
    local_proj = jnp.dot(
        signs, cross, precision=lax.Precision.HIGH, preferred_element_type=jnp.float32
    )
    lefts = [left for left, _, _ in panels(count)]
    parts = [outer_sum(cross[:, left:], cross[:, left:left + 256]) for left in lefts]
    parts.append(local_proj.reshape(-1, 256))
    total = sum_rows(jnp.concatenate(parts), "rows", size, 3, 2)
    packed = panels(count)[-1][2]
    kern = [
        kernel(landmarks[left:], landmarks[left:left + 256], land_sq[left:left + 256])
        for left in lefts
    ]
    kern = noise[0] * jnp.concatenate(kern)
    solved = solve_rows(total[:packed], kern, total[packed:].reshape(local_proj.shape))
    return (signs - mm_nt(solved, cross)) / noise[0]


def solution(mesh):
    in_specs = (P(("groups", "rows"), None), P("groups"), P(), P(), P(None, ("groups", "rows")))
    out_specs = P(None, ("groups", "rows"))
    return jax.shard_map(functools.partial(local, mesh.shape["rows"]), mesh=mesh, in_specs=in_specs, out_specs=out_specs, check_vma=False)
```
